32 devices in a mesh: groups: 2 (over x), inter: 2 (over core), intra: 8 (over z, y).
Axes of the slice: x: 2, y: 2, z: 4, core: 2. Of those that a mesh axis runs over, the one named last changes fastest.
Arguments:
- tokens: bfloat16 [192, 7168], P(('groups', 'inter', 'intra')), parts along dimension 0, may hold values from -6 to 6
- grad_out: bfloat16 [192, 7168], P(('groups', 'inter', 'intra')), parts along dimension 0, may hold values from -6 to 6
- gate_probs: float32 [192, 2], P(('groups', 'inter', 'intra')), parts along dimension 0, may hold values from 0.1 to 1
- routes: int32 [192, 2], P(('groups', 'inter', 'intra')), parts along dimension 0, may hold values from 0 to 3, all different within a row; in each aligned block of 6 rows (0 to 5, 6 to 11, ...) at most 5 rows name the same one
- w_gate: bfloat16 [4, 608, 7168], P('inter', 'intra'), may hold values from -0.0625 to 0.0625
- w_up: bfloat16 [4, 608, 7168], P('inter', 'intra'), may hold values from -0.0625 to 0.0625
- w_down: bfloat16 [4, 608, 7168], P('inter', 'intra'), may hold values from -0.25 to 0.25
Outputs:
- grad_tokens: bfloat16 [192, 7168], P(('groups', 'inter', 'intra')), parts along dimension 0
- grad_gate: bfloat16 [8, 608, 7168], P(('groups', 'inter'), 'intra'), parts along dimension 0
- grad_up: bfloat16 [8, 608, 7168], P(('groups', 'inter'), 'intra'), parts along dimension 0
- grad_down: bfloat16 [8, 608, 7168], P(('groups', 'inter'), 'intra'), parts along dimension 0
The draws below stay inside these ranges and needn't reach their ends.
There are 2 independent parts, one for each index of `groups`. The reference program is written for one: setup_inputs(seed, part) draws one part's arguments, and reference() takes and returns one part's arrays. A program takes and returns all parts, laid end to end along the dimension named above; an argument that names none is the same for every part. Nothing has to cross between parts.
Inputs may be any that keep to these rules, and one draw needn't show every extreme that they name: `routes`: the 2 experts of a token differ. Among the 6 tokens of one device no expert is named more than 5 times, and in every draw some device names some expert exactly 5 times.
All inputs are finite; a program needn't handle non-finite values.
Results may differ from the reference program's by a relative error of at most 0.014.
Values may be sent and summed in bfloat16 or wider, within the bound.
A program may use at most 192 MiB of HBM per device.

```python
import math
import jax
import jax.numpy as jnp
import numpy as np
from jax import lax

D = 7168
FF_SUB = 76
TOP = 2
TOK_DEV = 6
FLIGHT = 4
FF = 608
TOKENS = 96
CAP = 5
N_INTRA = 8


def block_levels(own_key, dims, pieces, low, high):
    def one(position, parts):
        draws = jax.random.uniform(jax.random.fold_in(jax.random.fold_in(own_key, 6), position), (parts,), jnp.float32, low / len(pieces), high / len(pieces))
        return jnp.repeat(jnp.exp(draws), dims[position] // parts).reshape((-1,) + (1,) * (len(dims) - position - 1))

    gain = one(*pieces[0])
    for cut in pieces[1:]:
        gain = gain * one(*cut)
    return gain


def assign_block(own_key, own, number, rows, number_of, top, limit, lean):
    sequence = jax.random.permutation(own_key, number_of)
    crowded, ordinary = portions_of(number_of, rows * top, limit, lean, True), portions_of(number_of, rows * top, limit, lean, False)
    places = jnp.arange(number_of)

    def named(lengths, rotation):
        used = int((lengths > 0).sum())
        fixed = max(1, used // 4)
        moved = fixed + (places - fixed + rotation * (used - fixed)) % max(1, number_of - fixed)
        return jnp.zeros((number_of,), jnp.int32).at[sequence[jnp.where(places < fixed, places, moved)]].set(jnp.asarray(lengths, jnp.int32))

    lengths = jnp.where(number % 4 == 0, named(crowded, number // 4), named(ordinary, number - number // 4 - 1))
    mixed = jax.random.permutation(jax.random.fold_in(own, 3), number_of)
    donor, receiver = mixed[0:number_of // 2 * 2:2], mixed[1:number_of // 2 * 2:2]
    slack = jnp.minimum(lengths[donor] - 1, limit - lengths[receiver]) // 2
    slack = jnp.where((donor == sequence[0]) | (receiver == sequence[0]) | (lengths[receiver] == 0), 0, jnp.maximum(slack, 0))
    moved = jax.random.randint(jax.random.fold_in(own, 4), (number_of // 2,), 0, 1 << 20) % (slack + 1)
    lengths = lengths.at[donor].add(-moved).at[receiver].add(moved)
    items = jnp.searchsorted(jnp.cumsum(lengths), jnp.arange(rows * top), side="right").astype(jnp.int32)
    table = items.reshape(top, rows).T
    table = table[jax.random.permutation(jax.random.fold_in(own, 1), rows)]
    rotation = jax.random.randint(jax.random.fold_in(own, 2), (rows, 1), 0, top)
    return jnp.take_along_axis(table, (jnp.arange(top)[None, :] + rotation) % top, axis=1)


def portions_of(amount, total, limit, lean, full):
    loads = [(1 << 20) // math.isqrt(grade ** lean) + 1 for grade in range(1, amount + 1)]
    largest = limit if full else min(limit, max(-(-total // amount), total * loads[0] // sum(loads)))
    least = 1 if total - largest >= amount - 1 else 0
    holding, spare = [largest] + [least] * (amount - 1), total - largest - least * (amount - 1)
    while spare > 0:
        movable = [i for i in range(1, amount) if holding[i] < largest] or [i for i in range(1, amount) if holding[i] < limit]
        mass, left = sum([loads[i] for i in movable]), spare
        for i in movable:
            extra = min(limit - holding[i], max(1, left * loads[i] // mass), spare)
            holding[i] = holding[i] + extra
            spare = spare - extra
    return np.array(holding)


def bell_draw(key, extent, width, limit, cuts=(), kind=jnp.bfloat16):
    loudness = block_levels(key, extent, cuts, -0.22, 0.18) if cuts else 1.0
    values = jax.random.normal(key, extent, jnp.float32) * width * loudness
    return jnp.minimum(jnp.maximum(values, -limit), limit).astype(kind)


def setup_inputs(seed: int = 0, part: int = 0) -> dict:
    seeds = jax.random.split(jax.random.key(seed), 8)
    part_splits = jax.random.split(jax.random.fold_in(seeds[7], part), 8)
    tokens = bell_draw(part_splits[0], (TOKENS, D), 1.0, 6.0, ((0, 16),))
    grad_out = bell_draw(part_splits[1], (TOKENS, D), 1.0, 6.0, ((0, 16),))
    gate_probs = jnp.clip(0.1 + 0.9 * jax.random.uniform(part_splits[2], (TOKENS, TOP), jnp.float32) ** block_levels(part_splits[2], (TOKENS, TOP), ((0, 16),), -0.2, 0.2), 0.1, 1.0)
    routes_keys = jax.random.split(jax.random.fold_in(part_splits[3], 1), TOKENS // TOK_DEV)
    routes_turns = jax.random.permutation(jax.random.fold_in(part_splits[3], 3), TOKENS // TOK_DEV)
    routes = jax.vmap(lambda own, number: assign_block(jax.random.fold_in(part_splits[3], 2), own, number, TOK_DEV, FLIGHT, TOP, CAP, 2))(routes_keys, routes_turns).reshape((TOKENS, TOP))
    w_gate = bell_draw(seeds[4], (FLIGHT, FF, D), D ** -0.5, 0.0625, ((0, 2), (1, 8)))
    w_up = bell_draw(seeds[5], (FLIGHT, FF, D), D ** -0.5, 0.0625, ((0, 2), (1, 8)))
    w_down = bell_draw(seeds[6], (FLIGHT, FF, D), FF ** -0.5, 0.25, ((0, 2), (1, 8)))
    return dict(tokens=tokens, grad_out=grad_out, gate_probs=gate_probs, routes=routes, w_gate=w_gate, w_up=w_up, w_down=w_down)


def add_block(total, block):
    pre_gate, pre_up, gate_block, up_block = block
    part = jnp.dot(pre_gate, gate_block, preferred_element_type=jnp.float32)
    part = part + jnp.dot(pre_up, up_block, preferred_element_type=jnp.float32)
    rounded = lax.optimization_barrier(part.astype(jnp.bfloat16))
    return total + rounded.astype(jnp.float32), None


def expert_pass(operands):
    expert_id, gate_w, up_w, down_w, pairs_x, pairs_dy, picks = operands
    chosen = (picks == expert_id)[:, None]
    rows_x = jnp.where(chosen, pairs_x, jnp.zeros_like(pairs_x))
    rows_dy = jnp.where(chosen, pairs_dy, jnp.zeros_like(pairs_dy))
    width_contract = (((1,), (1,)), ((), ()))
    gate = lax.dot_general(rows_x, gate_w, width_contract, preferred_element_type=jnp.float32)
    up = lax.dot_general(rows_x, up_w, width_contract, preferred_element_type=jnp.float32)
    sigma = jax.nn.sigmoid(gate)
    silu_gate = gate * sigma
    hidden = (silu_gate * up).astype(jnp.bfloat16)
    grad_hidden = lax.dot_general(rows_dy, down_w, width_contract, preferred_element_type=jnp.float32)
    grad_pre_gate = (grad_hidden * up * sigma * (1.0 + gate * (1.0 - sigma))).astype(jnp.bfloat16)
    grad_pre_up = (grad_hidden * silu_gate).astype(jnp.bfloat16)
    contract_rows = (((0,), (0,)), ((), ()))
    grad_down = lax.dot_general(hidden, rows_dy, contract_rows, preferred_element_type=jnp.float32).astype(jnp.bfloat16)
    grad_gate = lax.dot_general(grad_pre_gate, rows_x, contract_rows, preferred_element_type=jnp.float32).astype(jnp.bfloat16)
    grad_up = lax.dot_general(grad_pre_up, rows_x, contract_rows, preferred_element_type=jnp.float32).astype(jnp.bfloat16)
    n_pairs = rows_x.shape[0]
    pre_gate_blocks = jnp.transpose(grad_pre_gate.reshape(n_pairs, N_INTRA, FF_SUB), (1, 0, 2))
    pre_up_blocks = jnp.transpose(grad_pre_up.reshape(n_pairs, N_INTRA, FF_SUB), (1, 0, 2))
    gate_blocks = gate_w.reshape(N_INTRA, FF_SUB, D)
    up_blocks = up_w.reshape(N_INTRA, FF_SUB, D)
    start = jnp.zeros((n_pairs, D), jnp.float32)
    grad_rows, unused = lax.scan(add_block, start, (pre_gate_blocks, pre_up_blocks, gate_blocks, up_blocks))
    return grad_rows.astype(jnp.bfloat16), grad_gate, grad_up, grad_down


def reference(tokens, grad_out, gate_probs, routes, w_gate, w_up, w_down):
    n_pairs = TOKENS * TOP
    picks = routes.reshape(n_pairs).astype(jnp.int32)
    pairs_x = jnp.repeat(tokens, TOP, axis=0)
    scaled = (gate_probs[:, :, None].astype(jnp.float32) * grad_out[:, None, :].astype(jnp.float32)).astype(jnp.bfloat16)
    pairs_dy = scaled.reshape(n_pairs, D)
    expert_ids = jnp.arange(FLIGHT, dtype=jnp.int32)

    def one_expert(operands):
        expert_id, gate_w, up_w, down_w = operands
        return expert_pass((expert_id, gate_w, up_w, down_w, pairs_x, pairs_dy, picks))

    grad_rows, grad_gate, grad_up, grad_down = lax.map(one_expert, (expert_ids, w_gate, w_up, w_down))
    per_pair = jnp.sum(grad_rows.astype(jnp.float32), axis=0)
    grad_tokens = jnp.sum(per_pair.reshape(TOKENS, TOP, D), axis=1).astype(jnp.bfloat16)
    return grad_tokens, grad_gate, grad_up, grad_down
```

```python
import jax
import jax.numpy as jnp
from jax import lax
from jax.sharding import PartitionSpec as P

BOTH = ("inter", "intra")


def pair_weights(gate_probs, routes, n_flight):
    named = routes[:, :, None] == jnp.arange(n_flight, dtype=jnp.int32)[None, None, :]
    return jnp.sum(jnp.where(named, gate_probs[:, :, None], 0.0), axis=1)


def local(tokens, grad_out, gate_probs, routes, w_gate, w_up, w_down):
    tok_count, width = tokens.shape
    n_outer = lax.axis_size("inter")
    n_inner = lax.axis_size("intra")
    local_count = w_gate.shape[0]
    n_flight = local_count * n_outer
    total = n_outer * n_inner * tok_count
    weights = pair_weights(gate_probs, routes, n_flight)
    rows = jnp.concatenate([tokens, grad_out], axis=0)
    gathered = lax.all_gather(rows, BOTH, axis=0, tiled=False)
    weights = lax.all_gather(weights, BOTH, axis=0, tiled=True)
    x = gathered[:, :tok_count].reshape(total, width)
    dy = gathered[:, tok_count:].reshape(total, width)
    first = lax.axis_index("inter") * local_count
    mine = lax.dynamic_slice_in_dim(weights, first, local_count, axis=1).T[:, :, None]
    f32 = dict(preferred_element_type=jnp.float32)
    gate = jnp.einsum("td,ehd->eth", x, w_gate, **f32)
    up = jnp.einsum("td,ehd->eth", x, w_up, **f32)
    grad_hidden = mine * jnp.einsum("td,ehd->eth", dy, w_down, **f32)
    sigma = jax.nn.sigmoid(gate)
    silu_gate = gate * sigma
    hidden = (mine * silu_gate * up).astype(jnp.bfloat16)
    pre_gate = (grad_hidden * up * sigma * (1.0 + gate * (1.0 - sigma))).astype(jnp.bfloat16)
    pre_up = (grad_hidden * silu_gate).astype(jnp.bfloat16)
    part = jnp.einsum("eth,ehd->td", pre_gate, w_gate, **f32)
    part = part + jnp.einsum("eth,ehd->td", pre_up, w_up, **f32)
    grad_tokens = lax.psum_scatter(
        part.astype(jnp.bfloat16), BOTH, scatter_dimension=0, tiled=True
    )
    grad_down = jnp.einsum("eth,td->ehd", hidden, dy, **f32).astype(jnp.bfloat16)
    grad_gate = jnp.einsum("eth,td->ehd", pre_gate, x, **f32).astype(jnp.bfloat16)
    grad_up = jnp.einsum("eth,td->ehd", pre_up, x, **f32).astype(jnp.bfloat16)
    return (grad_tokens.astype(jnp.bfloat16), grad_gate, grad_up, grad_down)


def solution(mesh):
    row = P(("groups", "inter", "intra"), None)
    weight = P("inter", "intra", None)
    grad = P(("groups", "inter"), "intra", None)
    return jax.shard_map(
        local,
        mesh=mesh,
        in_specs=(row,) * 4 + (weight,) * 3,
        out_specs=(row, grad, grad, grad),
        check_vma=False,
    )
```

```python
import functools
import jax
import jax.numpy as jnp
from jax import lax
from jax.experimental import pallas as pl
from jax.experimental.pallas import tpu as pltpu
from jax.sharding import PartitionSpec as P

MESH = pl.DeviceIdType.MESH
SLOT_ROWS = 16
BACK_SPLIT = 8
COLUMN = 1024


def lanes_of(n_inner):
    return 2 if n_inner <= 8 else 1


def greet(peers):
    barrier = pltpu.get_barrier_semaphore()
    count = 0
    for condition, device in peers:
        if condition is None:
            pl.semaphore_signal(barrier, inc=1, device_id=device, device_id_type=MESH)
            count = count + 1
        else:

            @pl.when(condition)
            def _(device=device):
                pl.semaphore_signal(barrier, inc=1, device_id=device, device_id_type=MESH)

            count = count + jnp.where(condition, 1, 0)
    pl.semaphore_wait(barrier, count)


def gather_kernel(n_inner, rows_ref, out_ref, own_sem, up_sem, down_sem, side_sem, core_sem, recv_sem):
    n_y = lanes_of(n_inner)
    n_z = n_inner // n_y
    c = lax.axis_index("inter")
    j = lax.axis_index("intra")
    z, y = j // n_y, j % n_y
    has_up, has_down = z < n_z - 1, z > 0
    up = {"intra": j + n_y}
    down = {"intra": j - n_y}
    side = {"intra": z * n_y + (1 - y)}
    core = {"inter": 1 - c}
    peers = [(None, core), (has_up, up), (has_down, down)]
    if n_y == 2:
        peers.append((None, side))
    greet(peers)

    me = c * n_inner + j
    own = pltpu.make_async_copy(rows_ref, out_ref.at[me], own_sem)
    own.start()

    def copy(slot, sems, device, src=None):
        return pltpu.make_async_remote_copy(
            src_ref=out_ref.at[slot] if src is None else src,
            dst_ref=out_ref.at[slot],
            send_sem=sems.at[slot],
            recv_sem=recv_sem.at[slot],
            device_id=device,
            device_id_type=MESH,
        )

    def arrived(slot):
        copy(slot, core_sem, core).wait_recv()

    sent = []

    def send(condition, slot, sems, device, src=None):
        def go():
            copy(slot, sems, device, src).start()

        if condition is None:
            go()
        else:
            pl.when(condition)(go)
        sent.append((condition, slot, sems, device))

    send(has_up, me, up_sem, up, rows_ref)
    send(has_down, me, down_sem, down, rows_ref)
    if n_y == 2:
        send(None, me, side_sem, side, rows_ref)
    send(None, me, core_sem, core, rows_ref)

    def side_arrivals(k):
        for distance in (k, -k) if k else (0,):
            there = z + distance
            exists = (there >= 0) & (there < n_z) if k else None
            slot = c * n_inner + there * n_y + (1 - y)

            def go(slot=slot):
                arrived(slot)
                copy(slot, core_sem, core).start()

            if exists is None:
                go()
            else:
                pl.when(exists)(go)
            sent.append((exists, slot, core_sem, core))

    for k in range(1, n_z):
        for distance, onward, sems, device in (
            (-k, has_up, up_sem, up),
            (k, has_down, down_sem, down),
        ):
            there = z + distance
            exists = (there >= 0) & (there < n_z)
            slot = c * n_inner + there * n_y + y
            pl.when(exists)(functools.partial(arrived, slot))
            send(exists & onward, slot, sems, device)
            if n_y == 2:
                send(exists, slot, side_sem, side)
            send(exists, slot, core_sem, core)
        if n_y == 2:
            side_arrivals(k - 1)
    if n_y == 2:
        side_arrivals(n_z - 1)

    def last(i, carry):
        arrived((1 - c) * n_inner + i)
        return carry

    lax.fori_loop(0, n_inner, last, 0)
    own.wait()
    for condition, slot, sems, device in sent:
        done = copy(slot, sems, device).wait_send
        if condition is None:
            done()
        else:
            pl.when(condition)(done)


def gather_rows(rows, n_outer, n_inner):
    n = n_outer * n_inner
    return pl.pallas_call(
        functools.partial(gather_kernel, n_inner),
        out_shape=jax.ShapeDtypeStruct((n,) + rows.shape, rows.dtype),
        in_specs=[pl.BlockSpec(memory_space=pl.ANY)],
        out_specs=pl.BlockSpec(memory_space=pl.ANY),
        scratch_shapes=[pltpu.SemaphoreType.DMA(())] + [pltpu.SemaphoreType.DMA((n,))] * 5,
        compiler_params=pltpu.CompilerParams(collective_id=0, has_side_effects=True),
        name="gather_rows",
    )(rows)


def back_kernel(
    n_inner, part_ref, out_ref, core_got, kept, side_out, side_got, far_out, far_got,
    core_sem, core_rsem, side_sem, side_rsem, far_sem, far_rsem,
):
    n_y = lanes_of(n_inner)
    n_z = n_inner // n_y
    c = lax.axis_index("inter")
    j = lax.axis_index("intra")
    z, y = j // n_y, j % n_y
    core = {"inter": 1 - c}
    side = {"intra": z * n_y + (1 - y)}

    def far(k):
        return {"intra": ((z + k) % n_z) * n_y + y}

    peers = [(None, core)] + [(None, far(k)) for k in range(1, n_z)]
    if n_y == 2:
        peers.append((None, side))
    greet(peers)
    order = list(range(1, n_z)) + [0]

    def core_copy(k):
        there = (z + k) % n_z * n_y
        return pltpu.make_async_remote_copy(
            src_ref=part_ref.at[pl.ds((1 - c) * n_inner + there, n_y)],
            dst_ref=core_got.at[pl.ds(there, n_y)],
            send_sem=core_sem.at[k],
            recv_sem=core_rsem.at[k],
            device_id=core,
            device_id_type=MESH,
        )

    def side_copy(k):
        return pltpu.make_async_remote_copy(
            src_ref=side_out.at[k],
            dst_ref=side_got.at[k],
            send_sem=side_sem.at[k],
            recv_sem=side_rsem.at[k],
            device_id=side,
            device_id_type=MESH,
        )

    def far_copy(k):
        return pltpu.make_async_remote_copy(
            src_ref=far_out.at[k],
            dst_ref=far_got.at[k],
            send_sem=far_sem.at[k],
            recv_sem=far_rsem.at[k],
            device_id=far(k),
            device_id_type=MESH,
        )

    f32 = jnp.float32
    for k in order:
        core_copy(k).start()
    for k in order:
        core_copy(k).wait_recv()
        there = (z + k) % n_z * n_y

        def paired(lane):
            mine = part_ref[c * n_inner + there + lane].astype(f32)
            return mine + core_got[there + lane].astype(f32)

        if n_y == 2:
            side_out[k] = paired(1 - y).astype(jnp.bfloat16)
            side_copy(k).start()
        kept[k] = paired(y)
    for k in order:
        if n_y == 2:
            side_copy(k).wait_recv()
            kept[k] = kept[k] + side_got[k].astype(f32)
        if k:
            far_out[k] = kept[k].astype(jnp.bfloat16)
            far_copy(k).start()
    total = kept[0]
    for k in range(1, n_z):
        far_copy(k).wait_recv()
        total = total + far_got[k].astype(f32)
    out_ref[...] = total.astype(jnp.bfloat16)
    for k in order:
        core_copy(k).wait_send()
        if n_y == 2:
            side_copy(k).wait_send()
        if k:
            far_copy(k).wait_send()


def sum_back(part, n_inner):
    block = part.shape[1:]
    n_z = n_inner // lanes_of(n_inner)
    bf16 = jnp.bfloat16
    return pl.pallas_call(
        functools.partial(back_kernel, n_inner),
        out_shape=jax.ShapeDtypeStruct(block, bf16),
        in_specs=[pl.BlockSpec(memory_space=pltpu.VMEM)],
        out_specs=pl.BlockSpec(memory_space=pltpu.VMEM),
        scratch_shapes=[
            pltpu.VMEM((n_inner,) + block, bf16),
            pltpu.VMEM((n_z,) + block, jnp.float32),
        ]
        + [pltpu.VMEM((n_z,) + block, bf16)] * 4
        + [pltpu.SemaphoreType.DMA((n_z,))] * 6,
        compiler_params=pltpu.CompilerParams(
            collective_id=1, has_side_effects=True, vmem_limit_bytes=48 << 20
        ),
        name="sum_back",
    )(part)


def grads_kernel(left_ref, rows_ref, gate_ref, up_ref, down_ref):
    local_count = gate_ref.shape[0]
    rows = rows_ref[...]
    for number, out in enumerate((gate_ref, up_ref, down_ref)):
        for e in range(local_count):
            out[e] = jnp.dot(
                left_ref[number * local_count + e], rows, preferred_element_type=jnp.float32
            ).astype(jnp.bfloat16)


def weight_grads(left, rows, shape):
    local_count, hidden, width = shape
    step = COLUMN if width % COLUMN == 0 else width
    out = pl.BlockSpec((local_count, hidden, step), lambda i: (0, 0, i))
    return pl.pallas_call(
        grads_kernel,
        out_shape=[jax.ShapeDtypeStruct(shape, jnp.bfloat16)] * 3,
        grid=(width // step,),
        in_specs=[
            pl.BlockSpec(left.shape, lambda i: (0, 0, 0)),
            pl.BlockSpec((rows.shape[0], step), lambda i: (0, i)),
        ],
        out_specs=[out] * 3,
        compiler_params=pltpu.CompilerParams(vmem_limit_bytes=40 << 20),
        name="weight_grads",
    )(left, rows)


def three_parts(value):
    high = lax.reduce_precision(value, 8, 7)
    middle = lax.reduce_precision(value - high, 8, 7)
    low = value - high - middle
    return jnp.stack([high, middle, low]).astype(jnp.bfloat16)


def local(tokens, grad_out, gate_probs, routes, w_gate, w_up, w_down):
    tok_count, width = tokens.shape
    n_outer = lax.axis_size("inter")
    n_inner = lax.axis_size("intra")
    n = n_outer * n_inner
    local_count, hidden_count, _ = w_gate.shape
    n_flight = local_count * n_outer
    bf16 = jnp.bfloat16
    f32 = dict(preferred_element_type=jnp.float32)

    named = routes[:, :, None] == jnp.arange(n_flight, dtype=jnp.int32)[None, None, :]
    weights = jnp.sum(jnp.where(named, gate_probs[:, :, None], 0.0), axis=1)
    sent = three_parts(weights).reshape(1, 3 * tok_count * n_flight)
    spare = SLOT_ROWS - 2 * tok_count
    sent = jnp.pad(sent, ((0, spare - 1), (0, width - sent.shape[1])))
    rows = jnp.concatenate([tokens, grad_out, sent], axis=0)
    slots = gather_rows(rows, n_outer, n_inner)

    weights = slots[:, 2 * tok_count, : 3 * tok_count * n_flight].astype(jnp.float32)
    weights = jnp.sum(weights.reshape(n, 3, tok_count, n_flight), axis=1)
    first = lax.axis_index("inter") * local_count
    mine = lax.dynamic_slice_in_dim(weights, first, local_count, axis=2)
    mine = jnp.transpose(mine, (2, 0, 1))[:, :, :, None]
    flat = slots.reshape(n * SLOT_ROWS, width)

    def project(w, begin):
        whole = jnp.einsum("td,ehd->eth", flat, w, **f32)
        whole = whole.reshape(local_count, n, SLOT_ROWS, hidden_count)
        return whole[:, :, begin : begin + tok_count]

    gate = project(w_gate, 0)
    up = project(w_up, 0)
    grad_hidden = mine * project(w_down, tok_count)
    sigma = jax.nn.sigmoid(gate)
    silu_gate = gate * sigma
    hidden = (mine * silu_gate * up).astype(bf16)
    pre_gate = (grad_hidden * up * sigma * (1.0 + gate * (1.0 - sigma))).astype(bf16)
    pre_up = (grad_hidden * silu_gate).astype(bf16)

    compact = (local_count, n * tok_count, hidden_count)
    part = jnp.einsum("eth,ehd->td", pre_gate.reshape(compact), w_gate, **f32)
    part = part + jnp.einsum("eth,ehd->td", pre_up.reshape(compact), w_up, **f32)
    part = part.astype(bf16).reshape(n, tok_count, BACK_SPLIT, width // BACK_SPLIT)
    part = jnp.transpose(part, (0, 2, 1, 3)).reshape(n, BACK_SPLIT * tok_count, -1)
    back = sum_back(part, n_inner).reshape(BACK_SPLIT, tok_count, width // BACK_SPLIT)
    grad_tokens = jnp.transpose(back, (1, 0, 2)).reshape(tok_count, width)

    def spread(value, begin):
        after = SLOT_ROWS - tok_count - begin
        value = jnp.pad(value, ((0, 0), (0, 0), (begin, after), (0, 0)))
        value = value.reshape(local_count, n * SLOT_ROWS, hidden_count)
        return jnp.transpose(value, (0, 2, 1))

    left = jnp.concatenate(
        [spread(pre_gate, 0), spread(pre_up, 0), spread(hidden, tok_count)], axis=0
    )
    grad_gate, grad_up, grad_down = weight_grads(left, flat, w_gate.shape)
    return (grad_tokens, grad_gate, grad_up, grad_down)


def solution(mesh):
    row = P(("groups", "inter", "intra"), None)
    weight = P("inter", "intra", None)
    grad = P(("groups", "inter"), "intra", None)
    return jax.shard_map(
        local,
        mesh=mesh,
        in_specs=(row,) * 4 + (weight,) * 3,
        out_specs=(row, grad, grad, grad),
        check_vma=False,
    )
```

```python
import functools
import jax
import jax.numpy as jnp
from jax import lax
from jax.experimental import pallas as pl
from jax.experimental.pallas import tpu as pltpu
from jax.sharding import PartitionSpec as P

MESH = pl.DeviceIdType.MESH
SLOT_ROWS = 16
BACK_SPLIT = 8
COLUMN = 1024
EXTRA = 128


def lanes_of(n_inner):
    return 2 if n_inner <= 8 else 1


def greet(peers):
    barrier = pltpu.get_barrier_semaphore()
    count = 0
    for condition, device in peers:
        if condition is None:
            pl.semaphore_signal(barrier, inc=1, device_id=device, device_id_type=MESH)
            count = count + 1
        else:

            @pl.when(condition)
            def _(device=device):
                pl.semaphore_signal(barrier, inc=1, device_id=device, device_id_type=MESH)

            count = count + jnp.where(condition, 1, 0)
    pl.semaphore_wait(barrier, count)


def forward_kernel(
    n_inner, rows_ref, gate_hbm, up_hbm, down_hbm, compact_ref, slots_out, left_ref, part_ref,
    slots, raw, flat_w, products,
    own_sem, raw_sem, out_sem, up_sem, down_sem, side_sem, core_sem, recv_sem,
):
    n_y = lanes_of(n_inner)
    n_z = n_inner // n_y
    n, _, _ = slots.shape
    hidden_count, local_count, width = gate_hbm.shape
    joint = hidden_count * local_count
    n_flight = local_count * (n // n_inner)
    tok_count = compact_ref.shape[0] // n
    f32, bf16 = jnp.float32, jnp.bfloat16
    c = lax.axis_index("inter")
    j = lax.axis_index("intra")
    z, y = j // n_y, j % n_y
    has_up, has_down = z < n_z - 1, z > 0
    up = {"intra": j + n_y}
    down = {"intra": j - n_y}
    side = {"intra": z * n_y + (1 - y)}
    core = {"inter": 1 - c}
    me = c * n_inner + j
    own = pltpu.make_async_copy(rows_ref, slots.at[me], own_sem)
    own.start()
    loads = [
        pltpu.make_async_copy(w, raw.at[i], raw_sem.at[i])
        for i, w in enumerate((gate_hbm, up_hbm, down_hbm))
    ]
    for load in loads:
        load.start()
    peers = [(None, core), (has_up, up), (has_down, down)]
    if n_y == 2:
        peers.append((None, side))
    greet(peers)

    def copy(slot, sems, device):
        return pltpu.make_async_remote_copy(
            src_ref=slots.at[slot],
            dst_ref=slots.at[slot],
            send_sem=sems.at[slot],
            recv_sem=recv_sem.at[slot],
            device_id=device,
            device_id_type=MESH,
        )

    def arrived(slot):
        copy(slot, core_sem, core).wait_recv()

    own.wait()
    pl.when(has_up)(copy(me, up_sem, up).start)
    pl.when(has_down)(copy(me, down_sem, down).start)
    if n_y == 2:
        copy(me, side_sem, side).start()
    copy(me, core_sem, core).start()

    step = COLUMN if width % COLUMN == 0 else width
    for i, load in enumerate(loads):
        load.wait()

        def lay(k, carry, i=i):
            cols = pl.ds(pl.multiple_of(k * step, step), step)
            flat_w[i, :, cols] = raw[i, :, :, cols].reshape(joint, step)
            return carry

        lax.fori_loop(0, width // step, lay, 0)

    reach = jnp.minimum(z, n_z - 1 - z)

    def nearest(i):
        k = (i + 1) // 2
        near = jnp.where(i % 2 == 0, z + k, z - k)
        far = jnp.where(z < n_z - 1 - z, i, n_z - 1 - i)
        return jnp.where(i <= 2 * reach, near, far)

    def visit(i, carry):
        @pl.when((i > 0) & (i < n_z))
        def _():
            there = nearest(i)
            slot = c * n_inner + there * n_y + y
            arrived(slot)
            pl.when((there < z) & has_up)(copy(slot, up_sem, up).start)
            pl.when((there > z) & has_down)(copy(slot, down_sem, down).start)
            if n_y == 2:
                copy(slot, side_sem, side).start()
            copy(slot, core_sem, core).start()

        @pl.when(i > 0)
        def _():
            there = nearest(i - 1)
            if n_y == 2:
                slot = c * n_inner + there * n_y + (1 - y)
                arrived(slot)
                copy(slot, core_sem, core).start()
            for lane in range(n_y):
                arrived((1 - c) * n_inner + there * n_y + lane)
            places = [outer * n_inner + there * n_y for outer in range(n // n_inner)]
            rows = jnp.concatenate(
                [
                    slots[pl.ds(place, n_y), :, :width].reshape(n_y * SLOT_ROWS, width)
                    for place in places
                ],
                axis=0,
            )
            for w in range(3):
                product = lax.dot_general(
                    rows, flat_w[w], (((1,), (1,)), ((), ())), preferred_element_type=f32
                ).reshape(len(places), n_y, SLOT_ROWS, joint)
                for at, place in enumerate(places):
                    products[w, pl.ds(place, n_y)] = product[at]

        return carry

    lax.fori_loop(0, n_z + 1, visit, 0)
    save = pltpu.make_async_copy(slots, slots_out, out_sem)
    save.start()

    total = n * SLOT_ROWS
    extra = slots[:, :, width:].reshape(total, slots.shape[2] - width).astype(f32)
    lane = lax.broadcasted_iota(jnp.int32, extra.shape, 1)
    column = lax.broadcasted_iota(jnp.int32, (total, joint), 1)
    weight = jnp.zeros((total, joint), f32)
    for e in range(local_count):
        number = c * local_count + e
        named = (lane == number) | (lane == n_flight + number) | (lane == 2 * n_flight + number)
        one = jnp.sum(jnp.where(named, extra, 0.0), axis=1, keepdims=True)
        weight = jnp.where(column % local_count == e, one, weight)
    gate = products[0].reshape(total, joint)
    raised = products[1].reshape(total, joint)
    grad_hidden = products[2].reshape(total, joint)
    grad_hidden = weight * pltpu.roll(grad_hidden, total - tok_count, 0)
    sigma = jax.nn.sigmoid(gate)
    silu_gate = gate * sigma
    hidden = pltpu.roll(weight * silu_gate * raised, tok_count, 0)
    pre_gate = grad_hidden * raised * sigma * (1.0 + gate * (1.0 - sigma))
    pre_up = grad_hidden * silu_gate
    for i, value in enumerate((pre_gate, pre_up, hidden)):
        left_ref[i] = value.T.astype(bf16)
    compact = compact_ref[...]
    few = [
        jnp.dot(compact, value.astype(bf16), preferred_element_type=f32).astype(bf16)
        for value in (pre_gate, pre_up)
    ]
    for k in range(width // step):
        cols = slice(k * step, (k + 1) * step)
        part = jnp.dot(few[0], flat_w[0, :, cols], preferred_element_type=f32)
        part = part + jnp.dot(few[1], flat_w[1, :, cols], preferred_element_type=f32)
        part_ref[:, cols] = part.astype(bf16)

    def sent(i, carry):
        there = nearest(i)
        slot = c * n_inner + there * n_y + y
        pl.when((there <= z) & has_up)(copy(slot, up_sem, up).wait_send)
        pl.when((there >= z) & has_down)(copy(slot, down_sem, down).wait_send)
        copy(slot, core_sem, core).wait_send()
        if n_y == 2:
            copy(slot, side_sem, side).wait_send()
            slot = c * n_inner + there * n_y + (1 - y)
            copy(slot, core_sem, core).wait_send()
        return carry

    lax.fori_loop(0, n_z, sent, 0)
    save.wait()


def forward(rows, weights, n_outer, n_inner, tok_count):
    n = n_outer * n_inner
    hidden_count, local_count, width = weights[0].shape
    joint = hidden_count * local_count
    total = n * SLOT_ROWS
    bf16 = jnp.bfloat16
    there = jnp.arange(n * tok_count, dtype=jnp.int32)
    there = there // tok_count * SLOT_ROWS + there % tok_count
    compact = (there[:, None] == jnp.arange(total, dtype=jnp.int32)[None, :]).astype(bf16)
    anywhere, vmem = pl.BlockSpec(memory_space=pl.ANY), pl.BlockSpec(memory_space=pltpu.VMEM)
    slots = (n,) + rows.shape
    return pl.pallas_call(
        functools.partial(forward_kernel, n_inner),
        out_shape=[
            jax.ShapeDtypeStruct(slots, bf16),
            jax.ShapeDtypeStruct((3, joint, total), bf16),
            jax.ShapeDtypeStruct((n * tok_count, width), bf16),
        ],
        in_specs=[anywhere] * 4 + [vmem],
        out_specs=[anywhere, vmem, vmem],
        scratch_shapes=[
            pltpu.VMEM(slots, bf16),
            pltpu.VMEM((3,) + weights[0].shape, bf16),
            pltpu.VMEM((3, joint, width), bf16),
            pltpu.VMEM((3, n, SLOT_ROWS, joint), jnp.float32),
            pltpu.SemaphoreType.DMA(()),
            pltpu.SemaphoreType.DMA((3,)),
            pltpu.SemaphoreType.DMA(()),
        ]
        + [pltpu.SemaphoreType.DMA((n,))] * 5,
        compiler_params=pltpu.CompilerParams(
            collective_id=0, has_side_effects=True, vmem_limit_bytes=56 << 20
        ),
        name="forward",
    )(rows, *weights, compact)


def back_kernel(
    n_inner, part_ref, out_ref, core_got, kept, side_out, side_got, far_out, far_got,
    core_sem, core_rsem, side_sem, side_rsem, far_sem, far_rsem,
):
    n_y = lanes_of(n_inner)
    n_z = n_inner // n_y
    c = lax.axis_index("inter")
    j = lax.axis_index("intra")
    z, y = j // n_y, j % n_y
    core = {"inter": 1 - c}
    side = {"intra": z * n_y + (1 - y)}

    def far(k):
        return {"intra": ((z + k) % n_z) * n_y + y}

    peers = [(None, core)] + [(None, far(k)) for k in range(1, n_z)]
    if n_y == 2:
        peers.append((None, side))
    greet(peers)
    order = list(range(1, n_z)) + [0]

    def core_copy(k):
        there = (z + k) % n_z * n_y
        return pltpu.make_async_remote_copy(
            src_ref=part_ref.at[pl.ds((1 - c) * n_inner + there, n_y)],
            dst_ref=core_got.at[pl.ds(there, n_y)],
            send_sem=core_sem.at[k],
            recv_sem=core_rsem.at[k],
            device_id=core,
            device_id_type=MESH,
        )

    def side_copy(k):
        return pltpu.make_async_remote_copy(
            src_ref=side_out.at[k],
            dst_ref=side_got.at[k],
            send_sem=side_sem.at[k],
            recv_sem=side_rsem.at[k],
            device_id=side,
            device_id_type=MESH,
        )

    def far_copy(k):
        return pltpu.make_async_remote_copy(
            src_ref=far_out.at[k],
            dst_ref=far_got.at[k],
            send_sem=far_sem.at[k],
            recv_sem=far_rsem.at[k],
            device_id=far(k),
            device_id_type=MESH,
        )

    f32 = jnp.float32
    for k in order:
        core_copy(k).start()
    for k in order:
        core_copy(k).wait_recv()
        there = (z + k) % n_z * n_y

        def paired(lane):
            mine = part_ref[c * n_inner + there + lane].astype(f32)
            return mine + core_got[there + lane].astype(f32)

        if n_y == 2:
            side_out[k] = paired(1 - y).astype(jnp.bfloat16)
            side_copy(k).start()
        kept[k] = paired(y)
    for k in order:
        if n_y == 2:
            side_copy(k).wait_recv()
            kept[k] = kept[k] + side_got[k].astype(f32)
        if k:
            far_out[k] = kept[k].astype(jnp.bfloat16)
            far_copy(k).start()
    total = kept[0]
    for k in range(1, n_z):
        far_copy(k).wait_recv()
        total = total + far_got[k].astype(f32)
    out_ref[...] = total.astype(jnp.bfloat16)
    for k in order:
        core_copy(k).wait_send()
        if n_y == 2:
            side_copy(k).wait_send()
        if k:
            far_copy(k).wait_send()


def sum_back(part, n_inner):
    block = part.shape[1:]
    n_z = n_inner // lanes_of(n_inner)
    bf16 = jnp.bfloat16
    return pl.pallas_call(
        functools.partial(back_kernel, n_inner),
        out_shape=jax.ShapeDtypeStruct(block, bf16),
        in_specs=[pl.BlockSpec(memory_space=pltpu.VMEM)],
        out_specs=pl.BlockSpec(memory_space=pltpu.VMEM),
        scratch_shapes=[
            pltpu.VMEM((n_inner,) + block, bf16),
            pltpu.VMEM((n_z,) + block, jnp.float32),
        ]
        + [pltpu.VMEM((n_z,) + block, bf16)] * 4
        + [pltpu.SemaphoreType.DMA((n_z,))] * 6,
        compiler_params=pltpu.CompilerParams(
            collective_id=1, has_side_effects=True, vmem_limit_bytes=48 << 20
        ),
        name="sum_back",
    )(part)


def grads_kernel(left_ref, rows_ref, *outs):
    rows = rows_ref[...]
    for number, out in enumerate(outs):
        grad = jnp.dot(left_ref[number], rows, preferred_element_type=jnp.float32)
        out[...] = grad.astype(jnp.bfloat16).reshape(out.shape)


def weight_grads(left, rows, shape):
    hidden, local_count, width = shape
    step = COLUMN if width % COLUMN == 0 else width
    out = pl.BlockSpec((hidden, local_count, step), lambda i: (0, 0, i))
    return pl.pallas_call(
        grads_kernel,
        out_shape=[jax.ShapeDtypeStruct(shape, jnp.bfloat16)] * 3,
        grid=(width // step,),
        in_specs=[
            pl.BlockSpec(left.shape, lambda i: (0, 0, 0)),
            pl.BlockSpec((rows.shape[0], step), lambda i: (0, i)),
        ],
        out_specs=[out] * 3,
        compiler_params=pltpu.CompilerParams(vmem_limit_bytes=40 << 20),
        name="weight_grads",
    )(left, rows)


def three_parts(value):
    high = lax.reduce_precision(value, 8, 7)
    middle = lax.reduce_precision(value - high, 8, 7)
    low = value - high - middle
    return [part.astype(jnp.bfloat16) for part in (high, middle, low)]


def local(tokens, grad_out, gate_probs, routes, w_gate, w_up, w_down):
    tok_count, width = tokens.shape
    n_outer = lax.axis_size("inter")
    n_inner = lax.axis_size("intra")
    n = n_outer * n_inner
    n_flight = w_gate.shape[0] * n_outer

    named = routes[:, :, None] == jnp.arange(n_flight, dtype=jnp.int32)[None, None, :]
    weights = jnp.sum(jnp.where(named, gate_probs[:, :, None], 0.0), axis=1)
    extra = jnp.concatenate(three_parts(weights), axis=1)
    extra = jnp.pad(extra, ((0, SLOT_ROWS - tok_count), (0, EXTRA - extra.shape[1])))
    rows = jnp.concatenate([tokens, grad_out], axis=0)
    rows = jnp.pad(rows, ((0, SLOT_ROWS - 2 * tok_count), (0, 0)))
    rows = jnp.concatenate([rows, extra], axis=1)
    turned = [jnp.transpose(w, (1, 0, 2)) for w in (w_gate, w_up, w_down)]
    slots, left, part = forward(rows, turned, n_outer, n_inner, tok_count)

    part = part.reshape(n, tok_count, BACK_SPLIT, width // BACK_SPLIT)
    part = jnp.transpose(part, (0, 2, 1, 3)).reshape(n, BACK_SPLIT * tok_count, -1)
    back = sum_back(part, n_inner).reshape(BACK_SPLIT, tok_count, width // BACK_SPLIT)
    grad_tokens = jnp.transpose(back, (1, 0, 2)).reshape(tok_count, width)

    flat = slots.reshape(n * SLOT_ROWS, width + EXTRA)
    grads = weight_grads(left, flat, turned[0].shape)
    return (grad_tokens, *(jnp.transpose(grad, (1, 0, 2)) for grad in grads))


def solution(mesh):
    row = P(("groups", "inter", "intra"), None)
    weight = P("inter", "intra", None)
    grad = P(("groups", "inter"), "intra", None)
    return jax.shard_map(
        local,
        mesh=mesh,
        in_specs=(row,) * 4 + (weight,) * 3,
        out_specs=(row, grad, grad, grad),
        check_vma=False,
    )
```

```python
import functools
import jax
import jax.numpy as jnp
import numpy as np
from jax import lax
from jax.experimental import pallas as pl
from jax.experimental.pallas import tpu as pltpu
from jax.sharding import PartitionSpec as P

MESH = pl.DeviceIdType.MESH
SLOT_ROWS = 16
BACK_SPLIT = 8
COLUMN = 1024
EXTRA = 128
SEND_SPLIT = 4


def lanes_of(n_inner):
    return 2 if n_inner <= 8 else 1


def greet(peers):
    barrier = pltpu.get_barrier_semaphore()
    count = 0
    for condition, device in peers:
        if condition is None:
            pl.semaphore_signal(barrier, inc=1, device_id=device, device_id_type=MESH)
            count = count + 1
        else:

            @pl.when(condition)
            def _(device=device):
                pl.semaphore_signal(barrier, inc=1, device_id=device, device_id_type=MESH)

            count = count + jnp.where(condition, 1, 0)
    pl.semaphore_wait(barrier, count)


def forward_kernel(
    n_inner, tokens_ref, cotangent_ref, extra_ref, gate_hbm, up_hbm, down_hbm,
    slots_out, left_ref, part_ref, slots, wide, raw, flat_w, products, raw_sem, out_sem, up_sem, down_sem, side_sem, core_sem, recv_sem,
):
    n_y = lanes_of(n_inner)
    n_z = n_inner // n_y
    n, _, _ = slots.shape
    hidden_count, local_count, width = gate_hbm.shape
    joint = hidden_count * local_count
    n_flight = local_count * (n // n_inner)
    tok_count = tokens_ref.shape[0]
    both = 2 * tok_count
    piece = width // SEND_SPLIT
    f32, bf16 = jnp.float32, jnp.bfloat16
    c = lax.axis_index("inter")
    j = lax.axis_index("intra")
    z, y = j // n_y, j % n_y
    has_up, has_down = z < n_z - 1, z > 0
    up = {"intra": j + n_y}
    down = {"intra": j - n_y}
    side = {"intra": z * n_y + (1 - y)}
    core = {"inter": 1 - c}
    me = c * n_inner + j
    loads = [
        pltpu.make_async_copy(w, raw.at[i], raw_sem.at[i])
        for i, w in enumerate((gate_hbm, up_hbm, down_hbm))
    ]
    for load in loads:
        load.start()
    slots[me, :, piece:] = jnp.zeros((SEND_SPLIT * both, EXTRA), bf16)
    slots[me, :tok_count, piece:] = extra_ref[...]
    for q in range(SEND_SPLIT):
        cols = slice(q * piece, (q + 1) * piece)
        slots[me, q * both : q * both + tok_count, :piece] = tokens_ref[:, cols]
        slots[me, q * both + tok_count : (q + 1) * both, :piece] = cotangent_ref[:, cols]
    peers = [(None, core), (has_up, up), (has_down, down)]
    if n_y == 2:
        peers.append((None, side))
    greet(peers)

    def copy(slot, sems, device):
        return pltpu.make_async_remote_copy(
            src_ref=slots.at[slot],
            dst_ref=slots.at[slot],
            send_sem=sems.at[slot],
            recv_sem=recv_sem.at[slot],
            device_id=device,
            device_id_type=MESH,
        )

    def arrived(slot):
        copy(slot, core_sem, core).wait_recv()

    pl.when(has_up)(copy(me, up_sem, up).start)
    pl.when(has_down)(copy(me, down_sem, down).start)
    if n_y == 2:
        copy(me, side_sem, side).start()
    copy(me, core_sem, core).start()

    step = COLUMN if width % COLUMN == 0 else width
    for i, load in enumerate(loads):
        load.wait()

        def lay(k, carry, i=i):
            cols = pl.ds(pl.multiple_of(k * step, step), step)
            flat_w[i, :, cols] = raw[i, :, :, cols].reshape(joint, step)
            return carry

        lax.fori_loop(0, width // step, lay, 0)

    def clear(slot, carry):
        wide[slot] = jnp.zeros((SLOT_ROWS, width), bf16)
        return carry

    lax.fori_loop(0, n, clear, 0)
    reach = jnp.minimum(z, n_z - 1 - z)

    def nearest(i):
        k = (i + 1) // 2
        near = jnp.where(i % 2 == 0, z + k, z - k)
        far = jnp.where(z < n_z - 1 - z, i, n_z - 1 - i)
        return jnp.where(i <= 2 * reach, near, far)

    def visit(i, carry):
        @pl.when((i > 0) & (i < n_z))
        def _():
            there = nearest(i)
            slot = c * n_inner + there * n_y + y
            arrived(slot)
            pl.when((there < z) & has_up)(copy(slot, up_sem, up).start)
            pl.when((there > z) & has_down)(copy(slot, down_sem, down).start)
            if n_y == 2:
                copy(slot, side_sem, side).start()
            copy(slot, core_sem, core).start()

        @pl.when(i > 0)
        def _():
            there = nearest(i - 1)
            if n_y == 2:
                slot = c * n_inner + there * n_y + (1 - y)
                arrived(slot)
                copy(slot, core_sem, core).start()
            for lane in range(n_y):
                arrived((1 - c) * n_inner + there * n_y + lane)
            places = [outer * n_inner + there * n_y for outer in range(n // n_inner)]
            for place in places:
                for slot in range(n_y):
                    for q in range(SEND_SPLIT):
                        cols = slice(q * piece, (q + 1) * piece)
                        wide[place + slot, :both, cols] = slots[
                            place + slot, q * both : (q + 1) * both, :piece
                        ]
            rows = jnp.concatenate(
                [
                    wide[pl.ds(place, n_y)].reshape(n_y * SLOT_ROWS, width)
                    for place in places
                ],
                axis=0,
            )
            for w in range(3):
                product = lax.dot_general(
                    rows, flat_w[w], (((1,), (1,)), ((), ())), preferred_element_type=f32
                ).reshape(len(places), n_y, SLOT_ROWS, joint)
                for at, place in enumerate(places):
                    products[w, pl.ds(place, n_y)] = product[at]

        return carry

    lax.fori_loop(0, n_z + 1, visit, 0)
    save = pltpu.make_async_copy(wide, slots_out, out_sem)
    save.start()

    total = n * SLOT_ROWS
    extra = slots[:, :SLOT_ROWS, piece:].reshape(total, EXTRA).astype(f32)
    lane = lax.broadcasted_iota(jnp.int32, extra.shape, 1)
    column = lax.broadcasted_iota(jnp.int32, (total, joint), 1)
    weight = jnp.zeros((total, joint), f32)
    for e in range(local_count):
        number = c * local_count + e
        named = (lane == number) | (lane == n_flight + number) | (lane == 2 * n_flight + number)
        one = jnp.sum(jnp.where(named, extra, 0.0), axis=1, keepdims=True)
        weight = jnp.where(column % local_count == e, one, weight)
    gate = products[0].reshape(total, joint)
    raised = products[1].reshape(total, joint)
    grad_hidden = products[2].reshape(total, joint)
    grad_hidden = weight * pltpu.roll(grad_hidden, total - tok_count, 0)
    sigma = jax.nn.sigmoid(gate)
    silu_gate = gate * sigma
    hidden = pltpu.roll(weight * silu_gate * raised, tok_count, 0)
    pre_gate = grad_hidden * raised * sigma * (1.0 + gate * (1.0 - sigma))
    pre_up = grad_hidden * silu_gate
    for i, value in enumerate((pre_gate, pre_up, hidden)):
        left_ref[i] = value.T.astype(bf16)
    place = lax.broadcasted_iota(jnp.int32, (n * tok_count, total), 1)
    number = lax.broadcasted_iota(jnp.int32, (n * tok_count, total), 0)
    within = place % SLOT_ROWS
    compact = (place // SLOT_ROWS * tok_count + within == number) & (within < tok_count)
    compact = jnp.where(compact, 1.0, 0.0).astype(bf16)
    few = [
        jnp.dot(compact, value.astype(bf16), preferred_element_type=f32).astype(bf16)
        for value in (pre_gate, pre_up)
    ]
    for k in range(width // step):
        cols = slice(k * step, (k + 1) * step)
        part = jnp.dot(few[0], flat_w[0, :, cols], preferred_element_type=f32)
        part = part + jnp.dot(few[1], flat_w[1, :, cols], preferred_element_type=f32)
        part_ref[:, cols] = part.astype(bf16)

    def sent(i, carry):
        there = nearest(i)
        slot = c * n_inner + there * n_y + y
        pl.when((there <= z) & has_up)(copy(slot, up_sem, up).wait_send)
        pl.when((there >= z) & has_down)(copy(slot, down_sem, down).wait_send)
        copy(slot, core_sem, core).wait_send()
        if n_y == 2:
            copy(slot, side_sem, side).wait_send()
            slot = c * n_inner + there * n_y + (1 - y)
            copy(slot, core_sem, core).wait_send()
        return carry

    lax.fori_loop(0, n_z, sent, 0)
    save.wait()


def forward(tokens, grad_out, extra, weights, n_outer, n_inner):
    n = n_outer * n_inner
    tok_count = tokens.shape[0]
    hidden_count, local_count, width = weights[0].shape
    joint = hidden_count * local_count
    total = n * SLOT_ROWS
    bf16 = jnp.bfloat16
    anywhere, vmem = pl.BlockSpec(memory_space=pl.ANY), pl.BlockSpec(memory_space=pltpu.VMEM)
    slots = (n, SEND_SPLIT * 2 * tok_count, width // SEND_SPLIT + EXTRA)
    wide = (n, SLOT_ROWS, width)
    return pl.pallas_call(
        functools.partial(forward_kernel, n_inner),
        out_shape=[
            jax.ShapeDtypeStruct(wide, bf16),
            jax.ShapeDtypeStruct((3, joint, total), bf16),
            jax.ShapeDtypeStruct((n * tok_count, width), bf16),
        ],
        in_specs=[vmem] * 3 + [anywhere] * 3,
        out_specs=[anywhere, vmem, vmem],
        scratch_shapes=[
            pltpu.VMEM(slots, bf16),
            pltpu.VMEM(wide, bf16),
            pltpu.VMEM((3,) + weights[0].shape, bf16),
            pltpu.VMEM((3, joint, width), bf16),
            pltpu.VMEM((3, n, SLOT_ROWS, joint), jnp.float32),
            pltpu.SemaphoreType.DMA((3,)),
            pltpu.SemaphoreType.DMA(()),
        ]
        + [pltpu.SemaphoreType.DMA((n,))] * 5,
        compiler_params=pltpu.CompilerParams(
            collective_id=0, has_side_effects=True, vmem_limit_bytes=56 << 20
        ),
        name="forward",
    )(tokens, grad_out, extra, *weights)


def back_kernel(
    n_inner, part_ref, out_ref, core_got, kept, side_out, side_got, far_out, far_got,
    core_sem, core_rsem, side_sem, side_rsem, far_sem, far_rsem,
):
    n_y = lanes_of(n_inner)
    n_z = n_inner // n_y
    c = lax.axis_index("inter")
    j = lax.axis_index("intra")
    z, y = j // n_y, j % n_y
    core = {"inter": 1 - c}
    side = {"intra": z * n_y + (1 - y)}

    def far(k):
        return {"intra": ((z + k) % n_z) * n_y + y}

    peers = [(None, core)] + [(None, far(k)) for k in range(1, n_z)]
    if n_y == 2:
        peers.append((None, side))
    greet(peers)
    order = list(range(1, n_z)) + [0]

    def core_copy(k):
        there = (z + k) % n_z * n_y
        return pltpu.make_async_remote_copy(
            src_ref=part_ref.at[pl.ds((1 - c) * n_inner + there, n_y)],
            dst_ref=core_got.at[pl.ds(there, n_y)],
            send_sem=core_sem.at[k],
            recv_sem=core_rsem.at[k],
            device_id=core,
            device_id_type=MESH,
        )

    def side_copy(k):
        return pltpu.make_async_remote_copy(
            src_ref=side_out.at[k],
            dst_ref=side_got.at[k],
            send_sem=side_sem.at[k],
            recv_sem=side_rsem.at[k],
            device_id=side,
            device_id_type=MESH,
        )

    def far_copy(k):
        return pltpu.make_async_remote_copy(
            src_ref=far_out.at[k],
            dst_ref=far_got.at[k],
            send_sem=far_sem.at[k],
            recv_sem=far_rsem.at[k],
            device_id=far(k),
            device_id_type=MESH,
        )

    f32 = jnp.float32
    for k in order:
        core_copy(k).start()
    for k in order:
        core_copy(k).wait_recv()
        there = (z + k) % n_z * n_y

        def paired(lane):
            mine = part_ref[c * n_inner + there + lane].astype(f32)
            return mine + core_got[there + lane].astype(f32)

        if n_y == 2:
            side_out[k] = paired(1 - y).astype(jnp.bfloat16)
            side_copy(k).start()
        kept[k] = paired(y)
    for k in order:
        if n_y == 2:
            side_copy(k).wait_recv()
            kept[k] = kept[k] + side_got[k].astype(f32)
        if k:
            far_out[k] = kept[k].astype(jnp.bfloat16)
            far_copy(k).start()
    total = kept[0]
    for k in range(1, n_z):
        far_copy(k).wait_recv()
        total = total + far_got[k].astype(f32)
    out_ref[...] = total.astype(jnp.bfloat16)
    for k in order:
        core_copy(k).wait_send()
        if n_y == 2:
            side_copy(k).wait_send()
        if k:
            far_copy(k).wait_send()


def sum_back(part, n_inner):
    block = part.shape[1:]
    n_z = n_inner // lanes_of(n_inner)
    bf16 = jnp.bfloat16
    return pl.pallas_call(
        functools.partial(back_kernel, n_inner),
        out_shape=jax.ShapeDtypeStruct(block, bf16),
        in_specs=[pl.BlockSpec(memory_space=pltpu.VMEM)],
        out_specs=pl.BlockSpec(memory_space=pltpu.VMEM),
        scratch_shapes=[
            pltpu.VMEM((n_inner,) + block, bf16),
            pltpu.VMEM((n_z,) + block, jnp.float32),
        ]
        + [pltpu.VMEM((n_z,) + block, bf16)] * 4
        + [pltpu.SemaphoreType.DMA((n_z,))] * 6,
        compiler_params=pltpu.CompilerParams(
            collective_id=1, has_side_effects=True, vmem_limit_bytes=(8 + n_inner) << 20
        ),
        name="sum_back",
    )(part)


def grads_kernel(left_ref, rows_ref, *outs):
    rows = rows_ref[...]
    for number, out in enumerate(outs):
        grad = jnp.dot(left_ref[number], rows, preferred_element_type=jnp.float32)
        out[...] = grad.astype(jnp.bfloat16).reshape(out.shape)


def weight_grads(left, rows, shape):
    hidden, local_count, width = shape
    step = COLUMN if width % COLUMN == 0 else width
    out = pl.BlockSpec((hidden, local_count, step), lambda i: (0, 0, i))
    return pl.pallas_call(
        grads_kernel,
        out_shape=[jax.ShapeDtypeStruct(shape, jnp.bfloat16)] * 3,
        grid=(width // step,),
        in_specs=[
            pl.BlockSpec(left.shape, lambda i: (0, 0, 0)),
            pl.BlockSpec((rows.shape[0], step), lambda i: (0, i)),
        ],
        out_specs=[out] * 3,
        compiler_params=pltpu.CompilerParams(vmem_limit_bytes=40 << 20),
        name="weight_grads",
    )(left, rows)


def pair_columns(gate_probs, routes, n_flight):
    lane = np.arange(EXTRA, dtype=np.int32)[None, :]
    expert, which = lane % n_flight, lane // n_flight
    weights = 0.0
    for k in range(routes.shape[1]):
        weights = weights + jnp.where(routes[:, k : k + 1] == expert, gate_probs[:, k : k + 1], 0.0)
    high = lax.reduce_precision(weights, 8, 7)
    middle = lax.reduce_precision(weights - high, 8, 7)
    low = weights - high - middle
    picked = jnp.where(which == 0, high, jnp.where(which == 1, middle, low))
    return jnp.where(which < 3, picked, 0.0).astype(jnp.bfloat16)


def local(tokens, grad_out, gate_probs, routes, w_gate, w_up, w_down):
    tok_count, width = tokens.shape
    n_outer = lax.axis_size("inter")
    n_inner = lax.axis_size("intra")
    n = n_outer * n_inner
    n_flight = w_gate.shape[0] * n_outer

    extra = pair_columns(gate_probs, routes, n_flight)
    turned = [jnp.transpose(w, (1, 0, 2)) for w in (w_gate, w_up, w_down)]
    slots, left, part = forward(tokens, grad_out, extra, turned, n_outer, n_inner)

    part = part.reshape(n, tok_count, BACK_SPLIT, width // BACK_SPLIT)
    part = jnp.transpose(part, (0, 2, 1, 3)).reshape(n, BACK_SPLIT * tok_count, -1)
    back = sum_back(part, n_inner).reshape(BACK_SPLIT, tok_count, width // BACK_SPLIT)
    grad_tokens = jnp.transpose(back, (1, 0, 2)).reshape(tok_count, width)

    flat = slots.reshape(n * SLOT_ROWS, width)
    grads = weight_grads(left, flat, turned[0].shape)
    return (grad_tokens, *(jnp.transpose(grad, (1, 0, 2)) for grad in grads))


def solution(mesh):
    row = P(("groups", "inter", "intra"), None)
    weight = P("inter", "intra", None)
    grad = P(("groups", "inter"), "intra", None)
    return jax.shard_map(
        local,
        mesh=mesh,
        in_specs=(row,) * 4 + (weight,) * 3,
        out_specs=(row, grad, grad, grad),
        check_vma=False,
    )
```

```python
import functools
import jax
import jax.numpy as jnp
from jax import lax
from jax.experimental import pallas as pl
from jax.experimental.pallas import tpu as pltpu
from jax.sharding import PartitionSpec as P

MESH = pl.DeviceIdType.MESH
SLOT_ROWS = 16
BACK_SPLIT = 8
COLUMN = 1024
EXTRA = 128
SEND_SPLIT = 4


def lanes_of(n_inner):
    return 2 if n_inner <= 8 else 1


def greet(peers):
    barrier = pltpu.get_barrier_semaphore()
    count = 0
    for condition, device in peers:
        if condition is None:
            pl.semaphore_signal(barrier, inc=1, device_id=device, device_id_type=MESH)
            count = count + 1
        else:

            @pl.when(condition)
            def _(device=device):
                pl.semaphore_signal(barrier, inc=1, device_id=device, device_id_type=MESH)

            count = count + jnp.where(condition, 1, 0)
    pl.semaphore_wait(barrier, count)


def pair_columns(probs_ref, routes_ref, n_flight):
    f32, bf16 = jnp.float32, jnp.bfloat16
    top_k, tok_count = probs_ref.shape
    square = (tok_count, tok_count)
    same = lax.broadcasted_iota(jnp.int32, square, 0) == lax.broadcasted_iota(jnp.int32, square, 1)

    def upright(row):
        return jnp.sum(jnp.where(same, jnp.broadcast_to(row, square), 0.0), axis=1, keepdims=True)

    lane = lax.broadcasted_iota(jnp.int32, (tok_count, EXTRA), 1)
    expert, which = (lane % n_flight).astype(f32), lane // n_flight
    weights = jnp.zeros((tok_count, EXTRA), f32)
    for k in range(top_k):
        prob = upright(probs_ref[k : k + 1, :])
        route = upright(routes_ref[k : k + 1, :].astype(f32))
        weights = weights + jnp.where(route == expert, prob, 0.0)
    high = weights.astype(bf16).astype(f32)
    middle = (weights - high).astype(bf16).astype(f32)
    low = weights - high - middle
    picked = jnp.where(which == 0, high, jnp.where(which == 1, middle, low))
    return jnp.where(which < 3, picked, 0.0).astype(bf16)


def forward_kernel(
    n_inner, tokens_ref, cotangent_ref, probs_ref, routes_ref, gate_hbm, up_hbm, down_hbm,
    slots_out, left_ref, part_ref, slots, wide, raw, flat_w, products, raw_sem, out_sem, up_sem, down_sem, side_sem, core_sem, recv_sem,
):
    n_y = lanes_of(n_inner)
    n_z = n_inner // n_y
    n, _, _ = slots.shape
    hidden_count, local_count, width = gate_hbm.shape
    joint = hidden_count * local_count
    n_flight = local_count * (n // n_inner)
    tok_count = tokens_ref.shape[0]
    both = 2 * tok_count
    piece = width // SEND_SPLIT
    f32, bf16 = jnp.float32, jnp.bfloat16
    c = lax.axis_index("inter")
    j = lax.axis_index("intra")
    z, y = j // n_y, j % n_y
    has_up, has_down = z < n_z - 1, z > 0
    up = {"intra": j + n_y}
    down = {"intra": j - n_y}
    side = {"intra": z * n_y + (1 - y)}
    core = {"inter": 1 - c}
    me = c * n_inner + j
    loads = [
        pltpu.make_async_copy(w, raw.at[i], raw_sem.at[i])
        for i, w in enumerate((gate_hbm, up_hbm, down_hbm))
    ]
    for load in loads:
        load.start()
    slots[me, :, piece:] = jnp.zeros((SEND_SPLIT * both, EXTRA), bf16)
    slots[me, :tok_count, piece:] = pair_columns(probs_ref, routes_ref, n_flight)
    for q in range(SEND_SPLIT):
        cols = slice(q * piece, (q + 1) * piece)
        slots[me, q * both : q * both + tok_count, :piece] = tokens_ref[:, cols]
        slots[me, q * both + tok_count : (q + 1) * both, :piece] = cotangent_ref[:, cols]
    peers = [(None, core), (has_up, up), (has_down, down)]
    if n_y == 2:
        peers.append((None, side))
    greet(peers)

    def copy(slot, sems, device):
        return pltpu.make_async_remote_copy(
            src_ref=slots.at[slot],
            dst_ref=slots.at[slot],
            send_sem=sems.at[slot],
            recv_sem=recv_sem.at[slot],
            device_id=device,
            device_id_type=MESH,
        )

    def arrived(slot):
        copy(slot, core_sem, core).wait_recv()

    pl.when(has_up)(copy(me, up_sem, up).start)
    pl.when(has_down)(copy(me, down_sem, down).start)
    if n_y == 2:
        copy(me, side_sem, side).start()
    copy(me, core_sem, core).start()

    step = COLUMN if width % COLUMN == 0 else width
    for i, load in enumerate(loads):
        load.wait()

        def lay(k, carry, i=i):
            cols = pl.ds(pl.multiple_of(k * step, step), step)
            flat_w[i, :, cols] = raw[i, :, :, cols].reshape(joint, step)
            return carry

        lax.fori_loop(0, width // step, lay, 0)

    def clear(slot, carry):
        wide[slot] = jnp.zeros((SLOT_ROWS, width), bf16)
        return carry

    lax.fori_loop(0, n, clear, 0)
    reach = jnp.minimum(z, n_z - 1 - z)

    def nearest(i):
        k = (i + 1) // 2
        near = jnp.where(i % 2 == 0, z + k, z - k)
        far = jnp.where(z < n_z - 1 - z, i, n_z - 1 - i)
        return jnp.where(i <= 2 * reach, near, far)

    def visit(i, carry):
        @pl.when((i > 0) & (i < n_z))
        def _():
            there = nearest(i)
            slot = c * n_inner + there * n_y + y
            arrived(slot)
            pl.when((there < z) & has_up)(copy(slot, up_sem, up).start)
            pl.when((there > z) & has_down)(copy(slot, down_sem, down).start)
            if n_y == 2:
                copy(slot, side_sem, side).start()
            copy(slot, core_sem, core).start()

        @pl.when(i > 0)
        def _():
            there = nearest(i - 1)
            if n_y == 2:
                slot = c * n_inner + there * n_y + (1 - y)
                arrived(slot)
                copy(slot, core_sem, core).start()
            for lane in range(n_y):
                arrived((1 - c) * n_inner + there * n_y + lane)
            places = [outer * n_inner + there * n_y for outer in range(n // n_inner)]
            for place in places:
                for slot in range(n_y):
                    for q in range(SEND_SPLIT):
                        cols = slice(q * piece, (q + 1) * piece)
                        wide[place + slot, :both, cols] = slots[
                            place + slot, q * both : (q + 1) * both, :piece
                        ]
            rows = jnp.concatenate(
                [
                    wide[pl.ds(place, n_y)].reshape(n_y * SLOT_ROWS, width)
                    for place in places
                ],
                axis=0,
            )
            for w in range(3):
                product = lax.dot_general(
                    rows, flat_w[w], (((1,), (1,)), ((), ())), preferred_element_type=f32
                ).reshape(len(places), n_y, SLOT_ROWS, joint)
                for at, place in enumerate(places):
                    products[w, pl.ds(place, n_y)] = product[at]

        return carry

    lax.fori_loop(0, n_z + 1, visit, 0)
    save = pltpu.make_async_copy(wide, slots_out, out_sem)
    save.start()

    total = n * SLOT_ROWS
    extra = slots[:, :SLOT_ROWS, piece:].reshape(total, EXTRA).astype(f32)
    lane = lax.broadcasted_iota(jnp.int32, extra.shape, 1)
    column = lax.broadcasted_iota(jnp.int32, (total, joint), 1)
    weight = jnp.zeros((total, joint), f32)
    for e in range(local_count):
        number = c * local_count + e
        named = (lane == number) | (lane == n_flight + number) | (lane == 2 * n_flight + number)
        one = jnp.sum(jnp.where(named, extra, 0.0), axis=1, keepdims=True)
        weight = jnp.where(column % local_count == e, one, weight)
    gate = products[0].reshape(total, joint)
    raised = products[1].reshape(total, joint)
    grad_hidden = products[2].reshape(total, joint)
    grad_hidden = weight * pltpu.roll(grad_hidden, total - tok_count, 0)
    sigma = jax.nn.sigmoid(gate)
    silu_gate = gate * sigma
    hidden = pltpu.roll(weight * silu_gate * raised, tok_count, 0)
    pre_gate = grad_hidden * raised * sigma * (1.0 + gate * (1.0 - sigma))
    pre_up = grad_hidden * silu_gate
    for i, value in enumerate((pre_gate, pre_up, hidden)):
        left_ref[i] = value.T.astype(bf16)
    place = lax.broadcasted_iota(jnp.int32, (n * tok_count, total), 1)
    number = lax.broadcasted_iota(jnp.int32, (n * tok_count, total), 0)
    within = place % SLOT_ROWS
    compact = (place // SLOT_ROWS * tok_count + within == number) & (within < tok_count)
    compact = jnp.where(compact, 1.0, 0.0).astype(bf16)
    few = [
        jnp.dot(compact, value.astype(bf16), preferred_element_type=f32).astype(bf16)
        for value in (pre_gate, pre_up)
    ]
    for k in range(width // step):
        cols = slice(k * step, (k + 1) * step)
        part = jnp.dot(few[0], flat_w[0, :, cols], preferred_element_type=f32)
        part = part + jnp.dot(few[1], flat_w[1, :, cols], preferred_element_type=f32)
        part_ref[:, cols] = part.astype(bf16)

    def sent(i, carry):
        there = nearest(i)
        slot = c * n_inner + there * n_y + y
        pl.when((there <= z) & has_up)(copy(slot, up_sem, up).wait_send)
        pl.when((there >= z) & has_down)(copy(slot, down_sem, down).wait_send)
        copy(slot, core_sem, core).wait_send()
        if n_y == 2:
            copy(slot, side_sem, side).wait_send()
            slot = c * n_inner + there * n_y + (1 - y)
            copy(slot, core_sem, core).wait_send()
        return carry

    lax.fori_loop(0, n_z, sent, 0)
    save.wait()


def forward(tokens, grad_out, gate_probs, routes, weights, n_outer, n_inner):
    n = n_outer * n_inner
    tok_count = tokens.shape[0]
    hidden_count, local_count, width = weights[0].shape
    joint = hidden_count * local_count
    total = n * SLOT_ROWS
    bf16 = jnp.bfloat16
    anywhere, vmem = pl.BlockSpec(memory_space=pl.ANY), pl.BlockSpec(memory_space=pltpu.VMEM)
    slots = (n, SEND_SPLIT * 2 * tok_count, width // SEND_SPLIT + EXTRA)
    wide = (n, SLOT_ROWS, width)
    return pl.pallas_call(
        functools.partial(forward_kernel, n_inner),
        out_shape=[
            jax.ShapeDtypeStruct(wide, bf16),
            jax.ShapeDtypeStruct((3, joint, total), bf16),
            jax.ShapeDtypeStruct((n * tok_count, width), bf16),
        ],
        in_specs=[vmem] * 4 + [anywhere] * 3,
        out_specs=[anywhere, vmem, vmem],
        scratch_shapes=[
            pltpu.VMEM(slots, bf16),
            pltpu.VMEM(wide, bf16),
            pltpu.VMEM((3,) + weights[0].shape, bf16),
            pltpu.VMEM((3, joint, width), bf16),
            pltpu.VMEM((3, n, SLOT_ROWS, joint), jnp.float32),
            pltpu.SemaphoreType.DMA((3,)),
            pltpu.SemaphoreType.DMA(()),
        ]
        + [pltpu.SemaphoreType.DMA((n,))] * 5,
        compiler_params=pltpu.CompilerParams(
            collective_id=0, has_side_effects=True, vmem_limit_bytes=56 << 20
        ),
        name="forward",
    )(tokens, grad_out, gate_probs.T, routes.T, *weights)


def back_kernel(
    n_inner, part_ref, out_ref, core_got, kept, side_out, side_got, far_out, far_got,
    core_sem, core_rsem, side_sem, side_rsem, far_sem, far_rsem,
):
    n_y = lanes_of(n_inner)
    n_z = n_inner // n_y
    c = lax.axis_index("inter")
    j = lax.axis_index("intra")
    z, y = j // n_y, j % n_y
    core = {"inter": 1 - c}
    side = {"intra": z * n_y + (1 - y)}

    def far(k):
        return {"intra": ((z + k) % n_z) * n_y + y}

    peers = [(None, core)] + [(None, far(k)) for k in range(1, n_z)]
    if n_y == 2:
        peers.append((None, side))
    greet(peers)
    order = list(range(1, n_z)) + [0]

    def core_copy(k):
        there = (z + k) % n_z * n_y
        return pltpu.make_async_remote_copy(
            src_ref=part_ref.at[pl.ds((1 - c) * n_inner + there, n_y)],
            dst_ref=core_got.at[pl.ds(there, n_y)],
            send_sem=core_sem.at[k],
            recv_sem=core_rsem.at[k],
            device_id=core,
            device_id_type=MESH,
        )

    def side_copy(k):
        return pltpu.make_async_remote_copy(
            src_ref=side_out.at[k],
            dst_ref=side_got.at[k],
            send_sem=side_sem.at[k],
            recv_sem=side_rsem.at[k],
            device_id=side,
            device_id_type=MESH,
        )

    def far_copy(k):
        return pltpu.make_async_remote_copy(
            src_ref=far_out.at[k],
            dst_ref=far_got.at[k],
            send_sem=far_sem.at[k],
            recv_sem=far_rsem.at[k],
            device_id=far(k),
            device_id_type=MESH,
        )

    f32 = jnp.float32
    for k in order:
        core_copy(k).start()
    for k in order:
        core_copy(k).wait_recv()
        there = (z + k) % n_z * n_y

        def paired(lane):
            mine = part_ref[c * n_inner + there + lane].astype(f32)
            return mine + core_got[there + lane].astype(f32)

        if n_y == 2:
            side_out[k] = paired(1 - y).astype(jnp.bfloat16)
            side_copy(k).start()
        kept[k] = paired(y)
    for k in order:
        if n_y == 2:
            side_copy(k).wait_recv()
            kept[k] = kept[k] + side_got[k].astype(f32)
        if k:
            far_out[k] = kept[k].astype(jnp.bfloat16)
            far_copy(k).start()
    total = kept[0]
    for k in range(1, n_z):
        far_copy(k).wait_recv()
        total = total + far_got[k].astype(f32)
    out_ref[...] = total.astype(jnp.bfloat16)
    for k in order:
        core_copy(k).wait_send()
        if n_y == 2:
            side_copy(k).wait_send()
        if k:
            far_copy(k).wait_send()


def sum_back(part, n_inner):
    block = part.shape[1:]
    n_z = n_inner // lanes_of(n_inner)
    bf16 = jnp.bfloat16
    return pl.pallas_call(
        functools.partial(back_kernel, n_inner),
        out_shape=jax.ShapeDtypeStruct(block, bf16),
        in_specs=[pl.BlockSpec(memory_space=pltpu.VMEM)],
        out_specs=pl.BlockSpec(memory_space=pltpu.VMEM),
        scratch_shapes=[
            pltpu.VMEM((n_inner,) + block, bf16),
            pltpu.VMEM((n_z,) + block, jnp.float32),
        ]
        + [pltpu.VMEM((n_z,) + block, bf16)] * 4
        + [pltpu.SemaphoreType.DMA((n_z,))] * 6,
        compiler_params=pltpu.CompilerParams(
            collective_id=1, has_side_effects=True, vmem_limit_bytes=(8 + n_inner) << 20
        ),
        name="sum_back",
    )(part)


def grads_kernel(left_ref, rows_ref, *outs):
    rows = rows_ref[...]
    for number, out in enumerate(outs):
        grad = jnp.dot(left_ref[number], rows, preferred_element_type=jnp.float32)
        out[...] = grad.astype(jnp.bfloat16).reshape(out.shape)


def weight_grads(left, rows, shape):
    hidden, local_count, width = shape
    step = COLUMN if width % COLUMN == 0 else width
    out = pl.BlockSpec((hidden, local_count, step), lambda i: (0, 0, i))
    return pl.pallas_call(
        grads_kernel,
        out_shape=[jax.ShapeDtypeStruct(shape, jnp.bfloat16)] * 3,
        grid=(width // step,),
        in_specs=[
            pl.BlockSpec(left.shape, lambda i: (0, 0, 0)),
            pl.BlockSpec((rows.shape[0], step), lambda i: (0, i)),
        ],
        out_specs=[out] * 3,
        compiler_params=pltpu.CompilerParams(vmem_limit_bytes=60 << 20),
        name="weight_grads",
    )(left, rows)


def local(tokens, grad_out, gate_probs, routes, w_gate, w_up, w_down):
    tok_count, width = tokens.shape
    n_outer = lax.axis_size("inter")
    n_inner = lax.axis_size("intra")
    n = n_outer * n_inner

    turned = [jnp.transpose(w, (1, 0, 2)) for w in (w_gate, w_up, w_down)]
    slots, left, part = forward(
        tokens, grad_out, gate_probs, routes, turned, n_outer, n_inner
    )

    part = part.reshape(n, tok_count, BACK_SPLIT, width // BACK_SPLIT)
    part = jnp.transpose(part, (0, 2, 1, 3)).reshape(n, BACK_SPLIT * tok_count, -1)
    back = sum_back(part, n_inner).reshape(BACK_SPLIT, tok_count, width // BACK_SPLIT)
    grad_tokens = jnp.transpose(back, (1, 0, 2)).reshape(tok_count, width)

    flat = slots.reshape(n * SLOT_ROWS, width)
    grads = weight_grads(left, flat, turned[0].shape)
    return (grad_tokens, *(jnp.transpose(grad, (1, 0, 2)) for grad in grads))


def solution(mesh):
    row = P(("groups", "inter", "intra"), None)
    weight = P("inter", "intra", None)
    grad = P(("groups", "inter"), "intra", None)
    return jax.shard_map(
        local,
        mesh=mesh,
        in_specs=(row,) * 4 + (weight,) * 3,
        out_specs=(row, grad, grad, grad),
        check_vma=False,
    )
```
